32 devices in a mesh: row: 4 (over y, x), col: 8 (over z, core).
Axes of the slice: x: 2, y: 2, z: 4, core: 2. Of those that a mesh axis runs over, the one named last changes fastest.
Arguments:
- eigvecs: float32 [512, 65536], P('col', 'row'), may hold values from -6 to 6
- reflectors: float32 [3, 256, 65536], P(None, 'col', 'row'), may hold values from -0.0234375 to 0.0234375
- factors: float32 [3, 256, 256], P(None, 'col'), may hold values from -1 to 2, as said below
Outputs:
- transformed: float32 [512, 65536], P('col', 'row')
The draws below stay inside these ranges and needn't reach their ends.
Inputs may be any that keep to these rules, and one draw needn't show every extreme that they name: factors[b] is upper triangular with diagonal entries between 1 and 2.
All inputs are finite; a program needn't handle non-finite values.
Results may differ from the reference program's by a relative error of at most 0.00012.
Values sent between devices are 32-bit elements; how exact they have to be, the bound alone decides.
A program may use at most 128 MiB of HBM per device.

```python
import math
import jax
import jax.numpy as jnp
from jax import lax

N = 65536
NB = 256
BLOCKS = 3
K = 512


def draw_factors(key, part):
    key = jax.random.fold_in(key, 7)
    key_off, key_diag = jax.random.split(key)
    offdiag = jnp.clip(jax.random.normal(key_off, (BLOCKS, NB, NB), jnp.float32), -4.0, 4.0) / math.sqrt(NB)
    diagonal = jax.random.uniform(key_diag, (BLOCKS, NB), jnp.float32, 1.0, 2.0)
    rows_idx = lax.broadcasted_iota(jnp.int32, (NB, NB), 0)
    cols_idx = lax.broadcasted_iota(jnp.int32, (NB, NB), 1)
    upper = (cols_idx > rows_idx).astype(jnp.float32)
    unit = (cols_idx == rows_idx).astype(jnp.float32)
    return offdiag * upper + diagonal[:, :, None] * unit


def level_of(stream_key, extent, shards, least, largest):
    def one(dim, parts):
        heights = jax.random.uniform(jax.random.fold_in(jax.random.fold_in(stream_key, 6), dim), (parts,), jnp.float32, least / len(shards), largest / len(shards))
        return jnp.repeat(jnp.exp(heights), extent[dim] // parts).reshape((-1,) + (1,) * (len(extent) - dim - 1))

    level = one(*shards[0])
    for cut in shards[1:]:
        level = level * one(*cut)
    return level


def normal_values(stream_key, shape, spread, most, cuts=(), kind=jnp.bfloat16):
    result = jax.random.normal(stream_key, shape, jnp.float32) * spread
    if len(cuts) > 0:
        result = level_of(stream_key, shape, cuts, -0.22, 0.18) * result
    return jnp.clip(result, min=-most, max=most).astype(kind)


def setup_inputs(seed: int = 0) -> dict:
    key_of = jax.random.split(jax.random.key(seed), 4)
    eigvecs = normal_values(key_of[0], (K, N), 1.0, 6.0, ((0, 8), (1, 4)), jnp.float32)
    reflectors = normal_values(key_of[1], (BLOCKS, NB, N), N ** -0.5, 0.0234375, ((1, 8), (2, 4)), jnp.float32)
    factors = draw_factors(jax.random.fold_in(key_of[3], 71), 0)
    return {"eigvecs": eigvecs, "reflectors": reflectors, "factors": factors}


def reference(eigvecs, reflectors, factors):
    current = eigvecs
    for index in range(BLOCKS - 1, -1, -1):
        panel = reflectors[index]
        inner = lax.dot_general(current, panel, (((1,), (1,)), ((), ())), precision=lax.Precision.HIGHEST, preferred_element_type=jnp.float32)
        scaled = lax.dot_general(inner, factors[index], (((1,), (1,)), ((), ())), precision=lax.Precision.HIGHEST, preferred_element_type=jnp.float32)
        current = current - jnp.dot(scaled, panel, precision=lax.Precision.HIGHEST, preferred_element_type=jnp.float32)
    return current
```

```python
import functools

import jax
import jax.numpy as jnp
from jax import lax
from jax.experimental import pallas as pl
from jax.experimental.pallas import tpu as pltpu
from jax.sharding import PartitionSpec as P

MESH = pl.DeviceIdType.MESH
HIGHEST = lax.Precision.HIGHEST


def product(left, right):
    return lax.dot_general(
        left, right, (((1,), (0,)), ((), ())), precision=HIGHEST, preferred_element_type=jnp.float32
    )


def product_last(left, right):
    return lax.dot_general(
        left, right, (((1,), (1,)), ((), ())), precision=HIGHEST, preferred_element_type=jnp.float32
    )


def await_bytes(ref, sem):
    pltpu.make_async_copy(ref, ref, sem).wait()


def kernel(
    rows, cols, group, tile,
    eig_ref, refl_ref, fact_ref, out_ref,
    panel, cur, fact, inner, part, parts, mine, pieces, scaled,
    fact_send, fact_recv, cur_send, cur_recv, panel_send, panel_recv,
    part_send, part_recv, scal_send, scal_recv, out_send, out_recv,
):
    blocks, depth, extent = refl_ref.shape
    vectors = eig_ref.shape[0]
    width = extent // group
    members = rows * group
    height = vectors * group // members
    row, col = lax.axis_index("row"), lax.axis_index("col")
    team, seat = col // group, col % group
    rank = row * group + seat

    def remote(src, dst, send, recv, to):
        pltpu.make_async_remote_copy(
            src_ref=src, dst_ref=dst, send_sem=send, recv_sem=recv, device_id=to, device_id_type=MESH
        ).start()

    def member(step):
        other = (rank + step) % members
        return other, (other // group, team * group + other % group)

    def cut(index):
        return pl.ds(pl.multiple_of(index * width, width), width)

    def own(index, size):
        return pl.ds(pl.multiple_of(index * size, size), size)

    def outside(step):
        return ((team + 1) * group + (step + seat) % (cols - group)) % cols

    def inside(step):
        return team * group + (seat + step) % group

    barrier = pltpu.get_barrier_semaphore()

    @pl.loop(1, members)
    def _(step):
        pl.semaphore_signal(barrier, inc=1, device_id=member(step)[1], device_id_type=MESH)

    @pl.loop(0, cols - group)
    def _(step):
        pl.semaphore_signal(barrier, inc=1, device_id=(row, outside(step)), device_id_type=MESH)

    pl.semaphore_wait(barrier, members - 1 + cols - group)

    def send_panel(index, other):
        remote(
            refl_ref.at[index, :, cut(other % group)], panel.at[index, own(col, depth), :],
            panel_send.at[index], panel_recv.at[index], (row, other),
        )

    def send_fact(other):
        remote(fact_ref, fact.at[:, own(col, depth), :], fact_send, fact_recv, (row, other))

    @pl.loop(1, group)
    def _(step):
        other = inside(step)
        remote(
            eig_ref.at[:, cut(other % group)], cur.at[own(seat, vectors), :], cur_send, cur_recv, (row, other)
        )

    for index in range(blocks - 1, -1, -1):
        @pl.loop(0, cols - group)
        def _(step):
            send_panel(index, outside(step))

        @pl.loop(1, group)
        def _(step):
            send_panel(index, inside(step))

        pltpu.make_async_copy(
            refl_ref.at[index, :, cut(seat)], panel.at[index, own(col, depth), :], panel_recv.at[index]
        ).start()
        if index == blocks - 1:
            @pl.loop(0, cols - group)
            def _(step):
                send_fact(outside(step))

            @pl.loop(1, group)
            def _(step):
                send_fact(inside(step))

            pltpu.make_async_copy(fact_ref, fact.at[:, own(col, depth), :], fact_recv).start()
            pltpu.make_async_copy(eig_ref.at[:, cut(seat)], cur.at[own(seat, vectors), :], cur_recv).start()

    await_bytes(cur, cur_recv)
    for index in range(blocks - 1, -1, -1):
        await_bytes(panel.at[index], panel_recv.at[index])
        inner[...] = jnp.zeros_like(inner)

        @pl.loop(0, width // tile)
        def _(step):
            at = pl.ds(pl.multiple_of(step * tile, tile), tile)
            inner[...] += product_last(cur[:, at], panel[index, :, at])

        for other in range(members):
            part[index, other] = inner[pl.ds(other * height, height), :]

        @pl.loop(1, members)
        def _(step):
            other, to = member(step)
            remote(part.at[index, other], parts.at[index, rank], part_send.at[index], part_recv.at[index], to)

        pltpu.make_async_copy(part.at[index, rank], parts.at[index, rank], part_recv.at[index]).start()
        if index == blocks - 1:
            await_bytes(fact, fact_recv)
        await_bytes(parts.at[index], part_recv.at[index])
        total = parts[index, 0]
        for other in range(1, members):
            total = total + parts[index, other]
        mine[index] = product_last(total, fact[index])

        @pl.loop(1, members)
        def _(step):
            remote(
                mine.at[index], pieces.at[index, rank], scal_send.at[index], scal_recv.at[index], member(step)[1]
            )

        pltpu.make_async_copy(mine.at[index], pieces.at[index, rank], scal_recv.at[index]).start()
        await_bytes(pieces.at[index], scal_recv.at[index])
        for other in range(members):
            scaled[pl.ds(other * height, height), :] = pieces[index, other]

        @pl.loop(0, width // tile)
        def _(step):
            at = pl.ds(pl.multiple_of(step * tile, tile), tile)
            cur[:, at] = cur[:, at] - product(scaled[...], panel[index, :, at])
            if index == 0:
                to_at = pl.ds(pl.multiple_of(seat * width + step * tile, tile), tile)

                @pl.loop(1, group)
                def _(hop):
                    other = inside(hop)
                    remote(
                        cur.at[own(other % group, vectors), at], out_ref.at[:, to_at], out_send, out_recv,
                        (row, other),
                    )

                pltpu.make_async_copy(cur.at[own(seat, vectors), at], out_ref.at[:, to_at], out_recv).start()

    await_bytes(out_ref, out_recv)
    await_bytes(cur.at[pl.ds(0, (group - 1) * vectors), :], out_send)
    await_bytes(cur.at[pl.ds(0, (group - 1) * vectors), :], cur_send)
    await_bytes(fact.at[:, pl.ds(0, (cols - 1) * depth), :], fact_send)
    for index in range(blocks):
        await_bytes(panel.at[index, pl.ds(0, (cols - 1) * depth), :], panel_send.at[index])
        await_bytes(parts.at[index, pl.ds(0, members - 1)], part_send.at[index])
        await_bytes(pieces.at[index, pl.ds(0, members - 1)], scal_send.at[index])


def shards(rows, cols, eigvecs, reflectors, factors):
    vectors, extent = eigvecs.shape
    blocks, depth, _ = reflectors.shape
    order = depth * cols
    group = min(4, cols // 2)
    width = extent // group
    tile = min(512, width)
    members = rows * group
    height = vectors * group // members
    dma = pltpu.SemaphoreType.DMA
    anywhere = pl.BlockSpec(memory_space=pl.ANY)
    exchanged = (blocks, members, height, order)
    return pl.pallas_call(
        functools.partial(kernel, rows, cols, group, tile),
        out_shape=jax.ShapeDtypeStruct(eigvecs.shape, jnp.float32),
        in_specs=[anywhere] * 3,
        out_specs=anywhere,
        scratch_shapes=[
            pltpu.VMEM((blocks, order, width), jnp.float32),
            pltpu.VMEM((vectors * group, width), jnp.float32),
            pltpu.VMEM((blocks, order, order), jnp.float32),
            pltpu.VMEM((vectors * group, order), jnp.float32),
            pltpu.VMEM(exchanged, jnp.float32),
            pltpu.VMEM(exchanged, jnp.float32),
            pltpu.VMEM((blocks, height, order), jnp.float32),
            pltpu.VMEM(exchanged, jnp.float32),
            pltpu.VMEM((vectors * group, order), jnp.float32),
            dma, dma, dma, dma, dma((blocks,)), dma((blocks,)),
            dma((blocks,)), dma((blocks,)), dma((blocks,)), dma((blocks,)), dma, dma,
        ],
        compiler_params=pltpu.CompilerParams(
            collective_id=0, has_side_effects=True, vmem_limit_bytes=52 * 1024 * 1024
        ),
        cost_estimate=pl.CostEstimate(
            flops=4 * blocks * vectors * group * order * width, bytes_accessed=4 * 6 * blocks * order * width,
            transcendentals=0,
        ),
    )(eigvecs, reflectors, factors)


def solution(mesh):
    placed = (P("col", "row"), P(None, "col", "row"), P(None, "col", None))
    return jax.shard_map(
        functools.partial(shards, mesh.shape["row"], mesh.shape["col"]),
        mesh=mesh, in_specs=placed, out_specs=P("col", "row"), check_vma=False,
    )
```

```python
import functools

import jax
import jax.numpy as jnp
from jax import lax
from jax.experimental import pallas as pl
from jax.experimental.pallas import tpu as pltpu
from jax.sharding import PartitionSpec as P

MESH = pl.DeviceIdType.MESH
HIGHEST = lax.Precision.HIGHEST


def split(value):
    high = value.astype(jnp.bfloat16)
    return high, (value - high.astype(jnp.float32)).astype(jnp.bfloat16)


def contract(left, right, dim):
    (left_high, left_low), (right_high, right_low) = split(left), split(right)

    def dot(one, other):
        return lax.dot_general(one, other, (((1,), (dim,)), ((), ())), preferred_element_type=jnp.float32)

    return dot(left_high, right_high) + (dot(left_high, right_low) + dot(left_low, right_high))


def product(left, right):
    return contract(left, right, 0)


def product_last(left, right):
    return contract(left, right, 1)


def await_bytes(ref, sem):
    pltpu.make_async_copy(ref, ref, sem).wait()


def factor_ways(rows, depth):
    return rows if depth % (8 * rows) == 0 else 1


def kernel(
    rows, cols, group, tile, slices,
    eig_ref, refl_ref, fact_ref, out_ref,
    panel, cur, fact, shares, inner, part, parts, mine, pieces, scaled,
    fact_send, fact_recv, share_send, share_recv, cur_send, cur_recv, panel_send, panel_recv,
    part_send, part_recv, scal_send, scal_recv, out_send, out_recv,
):
    blocks, depth, extent = refl_ref.shape
    vectors = eig_ref.shape[0]
    width = extent // group
    members = rows * group
    height = vectors * group // members
    row, col = lax.axis_index("row"), lax.axis_index("col")
    team, seat = col // group, col % group
    rank = row * group + seat
    ways = factor_ways(rows, depth)
    share = depth // ways
    way = row % ways
    slice_width = width // slices

    def remote(src, dst, send, recv, to):
        pltpu.make_async_remote_copy(
            src_ref=src, dst_ref=dst, send_sem=send, recv_sem=recv, device_id=to, device_id_type=MESH
        ).start()

    def member(step):
        other = (rank + step) % members
        return other, (other // group, team * group + other % group)

    def cut(index):
        return pl.ds(pl.multiple_of(index * width, width), width)

    def own(index, size):
        return pl.ds(pl.multiple_of(index * size, size), size)

    def outside(step):
        return ((team + 1) * group + (step + seat) % (cols - group)) % cols

    def inside(step):
        return team * group + (seat + step) % group

    barrier = pltpu.get_barrier_semaphore()

    @pl.loop(1, members)
    def _(step):
        pl.semaphore_signal(barrier, inc=1, device_id=member(step)[1], device_id_type=MESH)

    @pl.loop(0, cols - group)
    def _(step):
        pl.semaphore_signal(barrier, inc=1, device_id=(row, outside(step)), device_id_type=MESH)

    pl.semaphore_wait(barrier, members - 1 + cols - group)

    def parts_of(index):
        count = slices if index == 0 else 1
        return [(at, width // count) for at in range(count)]

    def panel_at(index, at, size):
        return panel.at[index, own(col, depth), pl.ds(at * size, size)]

    def panel_from(index, at, size, other):
        start = pl.multiple_of(other % group * width + at * size, size)
        return refl_ref.at[index, :, pl.ds(start, size)]

    def send_panel(index, at, size, other):
        remote(
            panel_from(index, at, size, other), panel_at(index, at, size),
            panel_send.at[index], panel_recv.at[index, at], (row, other),
        )

    def my_share():
        return fact_ref.at[:, own(way, share), :]

    def send_share(other):
        remote(my_share(), shares.at[way, :, col], fact_send, fact_recv, (row, other))

    @pl.loop(0, cols - group)
    def _(step):
        send_share(outside(step))

    @pl.loop(1, group)
    def _(step):
        send_share(inside(step))

    pltpu.make_async_copy(my_share(), shares.at[way, :, col], fact_recv).start()
    pltpu.make_async_copy(eig_ref.at[:, cut(seat)], cur.at[own(seat, vectors), :], cur_recv).start()

    for index in range(blocks - 1, -1, -1):
        for at, size in parts_of(index):
            @pl.loop(0, cols - group)
            def _(step):
                send_panel(index, at, size, outside(step))

            if index == blocks - 1:
                @pl.loop(1, group)
                def _(step):
                    other = inside(step)
                    remote(
                        eig_ref.at[:, cut(other % group)], cur.at[own(seat, vectors), :], cur_send, cur_recv,
                        (row, other),
                    )

            @pl.loop(1, group)
            def _(step):
                send_panel(index, at, size, inside(step))

            pltpu.make_async_copy(
                panel_from(index, at, size, col), panel_at(index, at, size), panel_recv.at[index, at]
            ).start()

    await_bytes(shares.at[way], fact_recv)
    if ways > 1:
        @pl.loop(1, ways)
        def _(step):
            remote(shares.at[way], shares.at[way], share_send, share_recv, ((row + step) % ways, col))

        await_bytes(shares.at[pl.ds(0, ways - 1)], share_recv)

    for index in range(blocks):
        for owner in range(cols):
            for at in range(ways):
                fact[index, pl.ds(owner * depth + at * share, share), :] = shares[at, index, owner]

    await_bytes(cur, cur_recv)
    for index in range(blocks - 1, -1, -1):
        inner[...] = jnp.zeros_like(inner)
        for number, size in parts_of(index):
            await_bytes(panel.at[index, :, pl.ds(number * size, size)], panel_recv.at[index, number])

            @pl.loop(0, size // tile)
            def _(step):
                at = pl.ds(pl.multiple_of(number * size + step * tile, tile), tile)
                inner[...] += product_last(cur[:, at], panel[index, :, at])

        for other in range(members):
            part[index, other] = inner[pl.ds(other * height, height), :]

        @pl.loop(1, members)
        def _(step):
            other, to = member(step)
            remote(part.at[index, other], parts.at[index, rank], part_send.at[index], part_recv.at[index], to)

        pltpu.make_async_copy(part.at[index, rank], parts.at[index, rank], part_recv.at[index]).start()
        await_bytes(parts.at[index], part_recv.at[index])
        total = parts[index, 0]
        for other in range(1, members):
            total = total + parts[index, other]
        mine[index] = product_last(total, fact[index])

        @pl.loop(1, members)
        def _(step):
            remote(
                mine.at[index], pieces.at[index, rank], scal_send.at[index], scal_recv.at[index], member(step)[1]
            )

        pltpu.make_async_copy(mine.at[index], pieces.at[index, rank], scal_recv.at[index]).start()
        await_bytes(pieces.at[index], scal_recv.at[index])
        for other in range(members):
            scaled[pl.ds(other * height, height), :] = pieces[index, other]

        @pl.loop(0, width // tile)
        def _(step):
            at = pl.ds(pl.multiple_of(step * tile, tile), tile)
            cur[:, at] = cur[:, at] - product(scaled[...], panel[index, :, at])
            if index == 0:
                to_at = pl.ds(pl.multiple_of(seat * width + step * tile, tile), tile)

                @pl.loop(1, group)
                def _(hop):
                    other = inside(hop)
                    remote(
                        cur.at[own(other % group, vectors), at], out_ref.at[:, to_at], out_send, out_recv,
                        (row, other),
                    )

                pltpu.make_async_copy(cur.at[own(seat, vectors), at], out_ref.at[:, to_at], out_recv).start()

    await_bytes(out_ref, out_recv)
    await_bytes(cur.at[pl.ds(0, (group - 1) * vectors), :], out_send)
    await_bytes(cur.at[pl.ds(0, (group - 1) * vectors), :], cur_send)
    await_bytes(shares.at[way, :, pl.ds(0, cols - 1)], fact_send)
    if ways > 1:
        await_bytes(shares.at[pl.ds(0, ways - 1)], share_send)
    for index in range(blocks):
        await_bytes(panel.at[index, pl.ds(0, (cols - 1) * depth), :], panel_send.at[index])
        await_bytes(parts.at[index, pl.ds(0, members - 1)], part_send.at[index])
        await_bytes(pieces.at[index, pl.ds(0, members - 1)], scal_send.at[index])


def shards(rows, cols, eigvecs, reflectors, factors):
    vectors, extent = eigvecs.shape
    blocks, depth, _ = reflectors.shape
    order = depth * cols
    group = min(4, cols // 2)
    width = extent // group
    tile = min(512, width)
    members = rows * group
    height = vectors * group // members
    dma = pltpu.SemaphoreType.DMA
    anywhere = pl.BlockSpec(memory_space=pl.ANY)
    ways = factor_ways(rows, depth)
    slices = max(1, min(4, width // tile))
    exchanged = (blocks, members, height, order)
    return pl.pallas_call(
        functools.partial(kernel, rows, cols, group, tile, slices),
        out_shape=jax.ShapeDtypeStruct(eigvecs.shape, jnp.float32),
        in_specs=[anywhere] * 3,
        out_specs=anywhere,
        scratch_shapes=[
            pltpu.VMEM((blocks, order, width), jnp.float32),
            pltpu.VMEM((vectors * group, width), jnp.float32),
            pltpu.VMEM((blocks, order, order), jnp.float32),
            pltpu.VMEM((ways, blocks, cols, depth // ways, order), jnp.float32),
            pltpu.VMEM((vectors * group, order), jnp.float32),
            pltpu.VMEM(exchanged, jnp.float32),
            pltpu.VMEM(exchanged, jnp.float32),
            pltpu.VMEM((blocks, height, order), jnp.float32),
            pltpu.VMEM(exchanged, jnp.float32),
            pltpu.VMEM((vectors * group, order), jnp.float32),
            dma, dma, dma, dma, dma, dma, dma((blocks,)), dma((blocks, slices)),
            dma((blocks,)), dma((blocks,)), dma((blocks,)), dma((blocks,)), dma, dma,
        ],
        compiler_params=pltpu.CompilerParams(
            collective_id=0, has_side_effects=True, vmem_limit_bytes=52 * 1024 * 1024
        ),
        cost_estimate=pl.CostEstimate(
            flops=4 * blocks * vectors * group * order * width, bytes_accessed=4 * 6 * blocks * order * width,
            transcendentals=0,
        ),
    )(eigvecs, reflectors, factors)


def solution(mesh):
    placed = (P("col", "row"), P(None, "col", "row"), P(None, "col", None))
    return jax.shard_map(
        functools.partial(shards, mesh.shape["row"], mesh.shape["col"]),
        mesh=mesh, in_specs=placed, out_specs=P("col", "row"), check_vma=False,
    )
```

```python
import functools

import jax
import jax.numpy as jnp
from jax import lax
from jax.experimental import pallas as pl
from jax.experimental.pallas import tpu as pltpu
from jax.sharding import PartitionSpec as P

MESH = pl.DeviceIdType.MESH
HIGHEST = lax.Precision.HIGHEST


def split(value):
    high = value.astype(jnp.bfloat16)
    return high, (value - high.astype(jnp.float32)).astype(jnp.bfloat16)


def contract(left, right, dim):
    (left_high, left_low), (right_high, right_low) = split(left), split(right)

    def dot(one, other):
        return lax.dot_general(one, other, (((1,), (dim,)), ((), ())), preferred_element_type=jnp.float32)

    return dot(left_high, right_high) + (dot(left_high, right_low) + dot(left_low, right_high))


def product(left, right):
    return contract(left, right, 0)


def product_last(left, right):
    return contract(left, right, 1)


def await_bytes(ref, sem):
    pltpu.make_async_copy(ref, ref, sem).wait()


def factor_ways(rows, depth):
    return rows if depth % (8 * rows) == 0 else 1


def kernel(
    rows, cols, group, tile, slices,
    eig_ref, refl_ref, fact_ref, out_ref,
    panel, cur, fact, shares, inner, part, parts, mine, pieces, scaled,
    fact_send, fact_recv, share_send, share_recv, cur_send, cur_recv, panel_send, panel_recv,
    part_send, part_recv, scal_send, scal_recv, out_send, out_recv,
):
    blocks, depth, extent = refl_ref.shape
    vectors = eig_ref.shape[0]
    width = extent // group
    members = rows * group
    height = vectors * group // members
    row, col = lax.axis_index("row"), lax.axis_index("col")
    team, seat = col // group, col % group
    rank = row * group + seat
    ways = factor_ways(rows, depth)
    share = depth // ways
    way = row % ways
    slice_width = width // slices

    def remote(src, dst, send, recv, to):
        pltpu.make_async_remote_copy(
            src_ref=src, dst_ref=dst, send_sem=send, recv_sem=recv, device_id=to, device_id_type=MESH
        ).start()

    def member(step):
        other = (rank + step) % members
        return other, (other // group, team * group + other % group)

    def cut(index):
        return pl.ds(pl.multiple_of(index * width, width), width)

    def own(index, size):
        return pl.ds(pl.multiple_of(index * size, size), size)

    def outside(step):
        return ((team + 1) * group + (step + seat) % (cols - group)) % cols

    def inside(step):
        return team * group + (seat + step) % group

    barrier = pltpu.get_barrier_semaphore()

    @pl.loop(1, members)
    def _(step):
        pl.semaphore_signal(barrier, inc=1, device_id=member(step)[1], device_id_type=MESH)

    @pl.loop(0, cols - group)
    def _(step):
        pl.semaphore_signal(barrier, inc=1, device_id=(row, outside(step)), device_id_type=MESH)

    pl.semaphore_wait(barrier, members - 1 + cols - group)

    def parts_of(index):
        count = slices if index == 0 else 1
        return [(at, width // count) for at in range(count)]

    def panel_at(index, at, size):
        return panel.at[index, own(col, depth), pl.ds(at * size, size)]

    def panel_from(index, at, size, other):
        start = pl.multiple_of(other % group * width + at * size, size)
        return refl_ref.at[index, :, pl.ds(start, size)]

    def send_panel(index, at, size, other):
        remote(
            panel_from(index, at, size, other), panel_at(index, at, size),
            panel_send.at[index], panel_recv.at[index, at], (row, other),
        )

    def my_share():
        return fact_ref.at[:, own(way, share), :]

    def send_share(other):
        remote(my_share(), shares.at[way, :, col], fact_send, fact_recv, (row, other))

    pltpu.make_async_copy(my_share(), shares.at[way, :, col], fact_recv).start()
    pltpu.make_async_copy(eig_ref.at[:, cut(seat)], cur.at[own(seat, vectors), :], cur_recv).start()

    for index in range(blocks - 1, -1, -1):
        for at, size in parts_of(index):
            @pl.loop(0, cols - group)
            def _(step):
                send_panel(index, at, size, outside(step))

            if index == blocks - 1:
                @pl.loop(0, cols - group)
                def _(step):
                    send_share(outside(step))

                @pl.loop(1, group)
                def _(step):
                    send_share(inside(step))

                @pl.loop(1, group)
                def _(step):
                    other = inside(step)
                    remote(
                        eig_ref.at[:, cut(other % group)], cur.at[own(seat, vectors), :], cur_send, cur_recv,
                        (row, other),
                    )

            @pl.loop(1, group)
            def _(step):
                send_panel(index, at, size, inside(step))

            pltpu.make_async_copy(
                panel_from(index, at, size, col), panel_at(index, at, size), panel_recv.at[index, at]
            ).start()

    await_bytes(shares.at[way], fact_recv)
    if ways > 1:
        @pl.loop(1, ways)
        def _(step):
            remote(shares.at[way], shares.at[way], share_send, share_recv, ((row + step) % ways, col))

        await_bytes(shares.at[pl.ds(0, ways - 1)], share_recv)

    for index in range(blocks):
        for owner in range(cols):
            for at in range(ways):
                fact[index, pl.ds(owner * depth + at * share, share), :] = shares[at, index, owner]

    await_bytes(cur, cur_recv)
    for index in range(blocks - 1, -1, -1):
        inner[...] = jnp.zeros_like(inner)
        for number, size in parts_of(index):
            await_bytes(panel.at[index, :, pl.ds(number * size, size)], panel_recv.at[index, number])

            @pl.loop(0, size // tile)
            def _(step):
                at = pl.ds(pl.multiple_of(number * size + step * tile, tile), tile)
                inner[...] += product_last(cur[:, at], panel[index, :, at])

        for other in range(members):
            part[index, other] = inner[pl.ds(other * height, height), :]

        @pl.loop(1, members)
        def _(step):
            other, to = member(step)
            remote(part.at[index, other], parts.at[index, rank], part_send.at[index], part_recv.at[index], to)

        pltpu.make_async_copy(part.at[index, rank], parts.at[index, rank], part_recv.at[index]).start()
        await_bytes(parts.at[index], part_recv.at[index])
        total = parts[index, 0]
        for other in range(1, members):
            total = total + parts[index, other]
        mine[index] = product_last(total, fact[index])

        @pl.loop(1, members)
        def _(step):
            remote(
                mine.at[index], pieces.at[index, rank], scal_send.at[index], scal_recv.at[index], member(step)[1]
            )

        pltpu.make_async_copy(mine.at[index], pieces.at[index, rank], scal_recv.at[index]).start()
        await_bytes(pieces.at[index], scal_recv.at[index])
        for other in range(members):
            scaled[pl.ds(other * height, height), :] = pieces[index, other]

        @pl.loop(0, width // tile)
        def _(step):
            at = pl.ds(pl.multiple_of(step * tile, tile), tile)
            cur[:, at] = cur[:, at] - product(scaled[...], panel[index, :, at])
            if index == 0:
                to_at = pl.ds(pl.multiple_of(seat * width + step * tile, tile), tile)

                @pl.loop(1, group)
                def _(hop):
                    other = inside(hop)
                    remote(
                        cur.at[own(other % group, vectors), at], out_ref.at[:, to_at], out_send, out_recv,
                        (row, other),
                    )

                pltpu.make_async_copy(cur.at[own(seat, vectors), at], out_ref.at[:, to_at], out_recv).start()

    await_bytes(out_ref, out_recv)
    await_bytes(cur.at[pl.ds(0, (group - 1) * vectors), :], out_send)
    await_bytes(cur.at[pl.ds(0, (group - 1) * vectors), :], cur_send)
    await_bytes(shares.at[way, :, pl.ds(0, cols - 1)], fact_send)
    if ways > 1:
        await_bytes(shares.at[pl.ds(0, ways - 1)], share_send)
    for index in range(blocks):
        await_bytes(panel.at[index, pl.ds(0, (cols - 1) * depth), :], panel_send.at[index])
        await_bytes(parts.at[index, pl.ds(0, members - 1)], part_send.at[index])
        await_bytes(pieces.at[index, pl.ds(0, members - 1)], scal_send.at[index])


def shards(rows, cols, eigvecs, reflectors, factors):
    vectors, extent = eigvecs.shape
    blocks, depth, _ = reflectors.shape
    order = depth * cols
    group = min(4, cols // 2)
    width = extent // group
    tile = min(1024, width)
    members = rows * group
    height = vectors * group // members
    dma = pltpu.SemaphoreType.DMA
    anywhere = pl.BlockSpec(memory_space=pl.ANY)
    ways = factor_ways(rows, depth)
    slices = max(1, min(4, width // tile))
    exchanged = (blocks, members, height, order)
    return pl.pallas_call(
        functools.partial(kernel, rows, cols, group, tile, slices),
        out_shape=jax.ShapeDtypeStruct(eigvecs.shape, jnp.float32),
        in_specs=[anywhere] * 3,
        out_specs=anywhere,
        scratch_shapes=[
            pltpu.VMEM((blocks, order, width), jnp.float32),
            pltpu.VMEM((vectors * group, width), jnp.float32),
            pltpu.VMEM((blocks, order, order), jnp.float32),
            pltpu.VMEM((ways, blocks, cols, depth // ways, order), jnp.float32),
            pltpu.VMEM((vectors * group, order), jnp.float32),
            pltpu.VMEM(exchanged, jnp.float32),
            pltpu.VMEM(exchanged, jnp.float32),
            pltpu.VMEM((blocks, height, order), jnp.float32),
            pltpu.VMEM(exchanged, jnp.float32),
            pltpu.VMEM((vectors * group, order), jnp.float32),
            dma, dma, dma, dma, dma, dma, dma((blocks,)), dma((blocks, slices)),
            dma((blocks,)), dma((blocks,)), dma((blocks,)), dma((blocks,)), dma, dma,
        ],
        compiler_params=pltpu.CompilerParams(
            collective_id=0, has_side_effects=True, vmem_limit_bytes=52 * 1024 * 1024
        ),
        cost_estimate=pl.CostEstimate(
            flops=4 * blocks * vectors * group * order * width, bytes_accessed=4 * 6 * blocks * order * width,
            transcendentals=0,
        ),
    )(eigvecs, reflectors, factors)


def solution(mesh):
    placed = (P("col", "row"), P(None, "col", "row"), P(None, "col", None))
    return jax.shard_map(
        functools.partial(shards, mesh.shape["row"], mesh.shape["col"]),
        mesh=mesh, in_specs=placed, out_specs=P("col", "row"), check_vma=False,
    )
```
